512 devices in a mesh: dp: 8 (over x, y_hi), fsdp: 64 (over z, y_lo, core).
Axes of the slice: x: 4, y: 8 (y_hi: 2, y_lo: 4; y = y_hi * 4 + y_lo), z: 8, core: 2. Of those that a mesh axis runs over, the one named last changes fastest.
Arguments:
- inputs: bfloat16 [16384, 4096], P('fsdp'), may hold values from -6 to 6
- grad_out: bfloat16 [16384, 14336], P('fsdp', 'dp'), may hold values from -0.3125 to 0.3125
- basis: bfloat16 [4096, 128], P(('dp', 'fsdp')), may hold values from -0.09375 to 0.09375
- moment_one: float32 [14336, 128], P(('dp', 'fsdp')), may hold values from -4 to 4
- moment_two: float32 [14336, 128], P(('dp', 'fsdp')), may hold values from 0.001 to 0.01
Outputs:
- moment_new: float32 [14336, 128], P(('dp', 'fsdp'))
- second_new: float32 [14336, 128], P(('dp', 'fsdp'))
- update: bfloat16 [4096, 14336], P(('dp', 'fsdp'))
The draws below stay inside these ranges and needn't reach their ends.
All inputs are finite; a program needn't handle non-finite values.
Results may differ from the reference program's by a relative error of at most 0.0085.
Values may be sent and summed in bfloat16 or wider, within the bound.
No kernel may reach another device: no remote copies, remote signals or barrier semaphores. Data moves between devices by JAX's collectives and lax.ppermute only.
A program may use at most 64 MiB of HBM per device.

```python
import math
import jax
import jax.numpy as jnp
from jax import lax

D = 4096
FF = 14336
R = 128
TOK_DEV = 256
TOKENS = 16384
N_FSDP = 64


def strengthened(array, own_key, source, target, parts, factor):
    def block_of(position):
        return (jnp.arange(array.shape[position]) // (array.shape[position] // parts)).reshape((-1,) + (1,) * (array.ndim - 1 - position))

    one_side = jax.random.permutation(own_key, parts)[block_of(target)]
    second = (block_of(target) + parts // 2) % parts
    return jnp.where((block_of(source) == one_side) | (block_of(source) == second), factor * array, array)


def block_levels(rng, dims, cuts, least, top_value):
    gain = 1.0
    for axis_at, blocks in cuts:
        draws = jax.random.uniform(jax.random.fold_in(jax.random.fold_in(rng, 6), axis_at), (blocks,), jnp.float32, least / len(cuts), top_value / len(cuts))
        gain = gain * jnp.repeat(jnp.exp(draws), dims[axis_at] // blocks).reshape((-1,) + (1,) * (len(dims) - 1 - axis_at))
    return gain


def scatter_about(key, extent, deviation, reach, split=(), held_as=jnp.bfloat16):
    array = deviation * jax.random.normal(key, extent, jnp.float32)
    if split:
        array = array * block_levels(key, extent, split, -0.22, 0.18)
    return jnp.clip(array, -reach, reach).astype(held_as)


def bell_draw_with(own_key, dims, spread, most, shards, heavy, kind=jnp.bfloat16):
    values = spread * jax.random.normal(own_key, dims, jnp.float32)
    if shards:
        values = values * block_levels(own_key, dims, shards, -0.22, 0.18)
    return jnp.clip(strengthened(values, jax.random.fold_in(own_key, 3), *heavy), -most, most).astype(kind)


def setup_inputs(seed: int = 0) -> dict:
    seeds = jax.random.split(jax.random.key(seed), 6)
    inputs = scatter_about(seeds[0], (TOKENS, D), 1.0, 6.0, ((0, 64),))
    grad_out = bell_draw_with(seeds[1], (TOKENS, FF), (TOKENS ** -0.5), 0.3125, ((0, 64), (1, 8)), (0, 1, 64, 4.0))
    basis = scatter_about(seeds[2], (D, R), D ** -0.5, 0.09375, ((0, 512),))
    moment_one = scatter_about(seeds[3], (FF, R), 0.3, 4.0, ((0, 512),), jnp.float32)
    moment_two = jnp.clip(jnp.exp(math.log(0.01) - 2.30258502 * jax.random.uniform(seeds[4], (FF, R), jnp.float32) ** block_levels(seeds[4], (FF, R), ((0, 512),), -0.2, 0.2)), 0.001, 0.01)
    return dict(inputs=inputs, grad_out=grad_out, basis=basis, moment_one=moment_one, moment_two=moment_two)


beta_one = 0.9
beta_two = 0.999
corr_one = 1.0 - 0.9 ** 20
corr_two = 1.0 - 0.999 ** 20
adam_eps = 1e-08

def reference(inputs, grad_out, basis, moment_one, moment_two):
    block_count = N_FSDP
    projected = jnp.dot(inputs, basis, preferred_element_type=jnp.float32).astype(jnp.bfloat16)
    proj_blocks = projected.reshape(block_count, TOK_DEV, R)
    grad_blocks = grad_out.reshape(block_count, TOK_DEV, FF)

    def add_block(total, pair):
        proj_piece, grad_piece = pair
        term = lax.dot_general(grad_piece, proj_piece, (((0,), (0,)), ((), ())), preferred_element_type=jnp.float32)
        rounded = lax.optimization_barrier(term.astype(jnp.bfloat16))
        return (total + rounded.astype(jnp.float32), None)
    gradient, unused = lax.scan(add_block, jnp.zeros((FF, R), jnp.float32), (proj_blocks, grad_blocks))
    moment_new = beta_one * moment_one + (1.0 - beta_one) * gradient
    second_new = beta_two * moment_two + (1.0 - beta_two) * gradient * gradient
    direction = (moment_new / corr_one / (jnp.sqrt(second_new / corr_two) + adam_eps)).astype(jnp.bfloat16)
    update = lax.dot_general(basis, direction, (((1,), (1,)), ((), ())), preferred_element_type=jnp.float32)
    return (moment_new, second_new, update.astype(jnp.bfloat16))
```

```python
import jax
import jax.numpy as jnp
from jax import lax
from jax.sharding import Mesh, PartitionSpec as P

beta_one = 0.9
beta_two = 0.999
corr_one = 1.0 - 0.9**20
corr_two = 1.0 - 0.999**20
adam_eps = 1e-08

bf16 = jnp.bfloat16
f32 = jnp.float32
DP = ("x", "yh")
FS = ("z", "yl", "c")
ALL = DP + FS
COL = ("yh", "z", "yl")


def spread(array, axes, count):
    return lax.all_to_all(jnp.broadcast_to(array, (count,) + array.shape), axes, 0, 0)


def shards(inputs, grad_out, basis, moment_one, moment_two):
    own_rows = spread(basis, COL, 64)
    mate_rows = lax.ppermute(own_rows, "c", [(0, 1), (1, 0)])
    first = lax.axis_index("c") == 0
    slab = jnp.concatenate(
        [jnp.where(first, own_rows, mate_rows), jnp.where(first, mate_rows, own_rows)], axis=1
    ).reshape(1024, 128)
    part = lax.dynamic_slice(inputs, (0, lax.axis_index("x") * 1024), (256, 1024))
    partial = jnp.dot(part, slab, preferred_element_type=f32).astype(bf16)
    projected = spread(partial, ("x",), 4).astype(f32).sum(0).astype(bf16)
    term = lax.dot_general(
        grad_out, projected, (((0,), (0,)), ((), ())), preferred_element_type=f32
    ).astype(bf16)
    pieces = lax.all_to_all(term.reshape(64, 28, 128), FS, 0, 0)
    gradient = pieces.astype(f32).sum(0)
    moment_new = beta_one * moment_one + (1.0 - beta_one) * gradient
    second_new = beta_two * moment_two + (1.0 - beta_two) * gradient * gradient
    direction = (moment_new / corr_one / (jnp.sqrt(second_new / corr_two) + adam_eps)).astype(bf16)
    near = spread(direction, ("x", "c"), 8).reshape(224, 128)
    block = lax.dot_general(
        own_rows.reshape(512, 128), near, (((1,), (1,)), ((), ())), preferred_element_type=f32
    ).astype(bf16)
    got = lax.all_to_all(block.reshape(64, 8, 224), COL, 0, 0)
    update = got.reshape(64, 8, 4, 56).transpose(1, 2, 0, 3).reshape(8, 14336)
    return (moment_new, second_new, update)


def solution(mesh):
    fine = Mesh(mesh.devices.reshape(4, 2, 8, 4, 2), ALL)
    in_specs = (P(FS, None), P(FS, DP), P(ALL, None), P(ALL, None), P(ALL, None))
    out_specs = (P(ALL, None), P(ALL, None), P(ALL, None))
    return jax.shard_map(shards, mesh=fine, in_specs=in_specs, out_specs=out_specs, check_vma=False)
```

```python
import jax
import jax.numpy as jnp
from jax import lax
from jax.sharding import Mesh, PartitionSpec as P

beta_one = 0.9
beta_two = 0.999
corr_one = 1.0 - 0.9**20
corr_two = 1.0 - 0.999**20
adam_eps = 1e-08

bf16 = jnp.bfloat16
f32 = jnp.float32
DP = ("x", "yh")
FS = ("z", "yl", "c")
ALL = DP + FS
COL = ("yh", "z", "yl")


def spread(array, axes, count):
    return lax.all_to_all(jnp.broadcast_to(array, (count,) + array.shape), axes, 0, 0)


def over_tokens(left, right):
    return lax.dot_general(left, right, (((0,), (0,)), ((), ())), preferred_element_type=f32)


def shards(inputs, grad_out, basis, moment_one, moment_two):
    mate_out = lax.ppermute(grad_out, "c", [(0, 1), (1, 0)])
    own_rows = spread(basis, COL, 64)
    slab = lax.all_gather(own_rows, "c", axis=1, tiled=True).reshape(1024, 128)
    part = lax.dynamic_slice(inputs, (0, lax.axis_index("x") * 1024), (256, 1024))
    partial = jnp.dot(part, slab, preferred_element_type=f32).astype(bf16)
    projected = spread(partial, ("x",), 4).astype(f32).sum(0).astype(bf16)
    both = lax.all_gather(projected, "c", axis=0)
    mate = lax.dynamic_index_in_dim(both, 1 - lax.axis_index("c"), 0, keepdims=False)
    term = over_tokens(grad_out, projected) + over_tokens(mate_out, mate)
    term = lax.dynamic_slice(
        term.astype(bf16).reshape(32, 56, 128), (0, lax.axis_index("c") * 28, 0), (32, 28, 128)
    )
    pieces = lax.all_to_all(term, ("z", "yl"), 0, 0)
    gradient = pieces.astype(f32).sum(0)
    moment_new = beta_one * moment_one + (1.0 - beta_one) * gradient
    second_new = beta_two * moment_two + (1.0 - beta_two) * gradient * gradient
    direction = (moment_new / corr_one / (jnp.sqrt(second_new / corr_two) + adam_eps)).astype(bf16)
    near = spread(direction, ("x", "c"), 8).reshape(224, 128)
    block = lax.dot_general(
        own_rows.reshape(512, 128), near, (((1,), (1,)), ((), ())), preferred_element_type=f32
    ).astype(bf16)
    got = lax.all_to_all(block.reshape(64, 8, 224), COL, 0, 0)
    update = got.reshape(64, 8, 4, 56).transpose(1, 2, 0, 3).reshape(8, 14336)
    return (moment_new, second_new, update)


def solution(mesh):
    fine = Mesh(mesh.devices.reshape(4, 2, 8, 4, 2), ALL)
    in_specs = (P(FS, None), P(FS, DP), P(ALL, None), P(ALL, None), P(ALL, None))
    out_specs = (P(ALL, None), P(ALL, None), P(ALL, None))
    return jax.shard_map(shards, mesh=fine, in_specs=in_specs, out_specs=out_specs, check_vma=False)
```

```python
import jax
import jax.numpy as jnp
from jax import lax
from jax.sharding import Mesh, PartitionSpec as P

beta_one = 0.9
beta_two = 0.999
corr_one = 1.0 - 0.9**20
corr_two = 1.0 - 0.999**20
adam_eps = 1e-08

bf16 = jnp.bfloat16
f32 = jnp.float32
DP = ("x", "yh")
FS = ("z", "yl", "c")
ALL = DP + FS
COL = ("yh", "z", "yl")


def spread(array, axes, count):
    return lax.all_to_all(jnp.broadcast_to(array, (count,) + array.shape), axes, 0, 0)


def over_tokens(left, right):
    return lax.dot_general(left, right, (((0,), (0,)), ((), ())), preferred_element_type=f32)


def shards(inputs, grad_out, basis, moment_one, moment_two):
    mate_out = lax.ppermute(grad_out, "c", [(0, 1), (1, 0)])
    own_rows = spread(basis, COL, 64)
    slab = lax.all_gather(own_rows, "c", axis=1, tiled=True).reshape(1024, 128)
    part = lax.dynamic_slice(inputs, (0, lax.axis_index("x") * 1024), (256, 1024))
    partial = jnp.dot(part, slab, preferred_element_type=f32).astype(bf16)
    partial, first = lax.optimization_barrier((partial, lax.axis_index("c") == 0))
    projected = spread(partial, ("x",), 4).astype(f32).sum(0).astype(bf16)
    both = lax.all_gather(projected, "c", axis=0)
    mate = jnp.where(first, both[1], both[0])
    term = (over_tokens(grad_out, projected) + over_tokens(mate_out, mate)).astype(bf16)
    term = term.reshape(32, 56, 128)
    term = jnp.where(first, term[:, :28], term[:, 28:])
    pieces = lax.all_to_all(term, ("z", "yl"), 0, 0)
    gradient = pieces.astype(f32).sum(0)
    moment_new = beta_one * moment_one + (1.0 - beta_one) * gradient
    second_new = beta_two * moment_two + (1.0 - beta_two) * gradient * gradient
    direction = (moment_new / corr_one / (jnp.sqrt(second_new / corr_two) + adam_eps)).astype(bf16)
    near = spread(direction, ("x", "c"), 8).reshape(224, 128)
    block = lax.dot_general(
        own_rows.reshape(512, 128), near, (((1,), (1,)), ((), ())), preferred_element_type=f32
    ).astype(bf16)
    got = lax.all_to_all(block.reshape(64, 8, 224), COL, 0, 0)
    update = got.reshape(64, 8, 4, 56).transpose(1, 2, 0, 3).reshape(8, 14336)
    return (moment_new, second_new, update)


def solution(mesh):
    fine = Mesh(mesh.devices.reshape(4, 2, 8, 4, 2), ALL)
    in_specs = (P(FS, None), P(FS, DP), P(ALL, None), P(ALL, None), P(ALL, None))
    out_specs = (P(ALL, None), P(ALL, None), P(ALL, None))
    return jax.shard_map(shards, mesh=fine, in_specs=in_specs, out_specs=out_specs, check_vma=False)
```

```python
import jax
import jax.numpy as jnp
from jax import lax
from jax.sharding import Mesh, PartitionSpec as P

beta_one = 0.9
beta_two = 0.999
corr_one = 1.0 - 0.9**20
corr_two = 1.0 - 0.999**20
adam_eps = 1e-08

bf16 = jnp.bfloat16
f32 = jnp.float32
DP = ("x", "yh")
FS = ("z", "yl", "c")
ALL = DP + FS
COL = ("yh", "z", "yl")


def spread(array, axes, count):
    return lax.all_to_all(jnp.broadcast_to(array, (count,) + array.shape), axes, 0, 0)


def over_tokens(left, right):
    return lax.dot_general(left, right, (((0,), (0,)), ((), ())), preferred_element_type=f32)


def shards(inputs, grad_out, basis, moment_one, moment_two):
    own_rows = spread(basis, COL, 64)
    cotangent = grad_out.T
    own_rows, cotangent = lax.optimization_barrier((own_rows, cotangent))
    slab = lax.all_gather(own_rows, "c", axis=1, tiled=True).reshape(1024, 128)
    part = lax.dynamic_slice(inputs, (0, lax.axis_index("x") * 1024), (256, 1024))
    partial = jnp.dot(part, slab, preferred_element_type=f32).astype(bf16)
    partial, first = lax.optimization_barrier((partial, lax.axis_index("c") == 0))
    projected = spread(partial, ("x",), 4).astype(f32).sum(0).astype(bf16)
    term = jnp.dot(cotangent, projected, preferred_element_type=f32).astype(bf16).reshape(32, 56, 128)
    even, odd = term[:, :28], term[:, 28:]
    pair = lax.all_gather(jnp.where(first, odd, even), "c", axis=0)
    term = jnp.where(first, even, odd).astype(f32) + jnp.where(first, pair[1], pair[0]).astype(f32)
    term = term.astype(bf16)
    pieces = lax.all_to_all(term, ("z", "yl"), 0, 0)
    gradient = pieces.astype(f32).sum(0)
    moment_new = beta_one * moment_one + (1.0 - beta_one) * gradient
    second_new = beta_two * moment_two + (1.0 - beta_two) * gradient * gradient
    direction = (moment_new / corr_one / (jnp.sqrt(second_new / corr_two) + adam_eps)).astype(bf16)
    near = spread(direction, ("x", "c"), 8).reshape(224, 128)
    block = lax.dot_general(
        own_rows.reshape(512, 128), near, (((1,), (1,)), ((), ())), preferred_element_type=f32
    ).astype(bf16)
    got = lax.all_to_all(block.reshape(64, 8, 224), COL, 0, 0)
    update = got.reshape(64, 8, 4, 56).transpose(1, 2, 0, 3).reshape(8, 14336)
    return (moment_new, second_new, update)


def solution(mesh):
    fine = Mesh(mesh.devices.reshape(4, 2, 8, 4, 2), ALL)
    in_specs = (P(FS, None), P(FS, DP), P(ALL, None), P(ALL, None), P(ALL, None))
    out_specs = (P(ALL, None), P(ALL, None), P(ALL, None))
    return jax.shard_map(shards, mesh=fine, in_specs=in_specs, out_specs=out_specs, check_vma=False)
```

```python
import jax
import jax.numpy as jnp
from jax import lax
from jax.sharding import Mesh, PartitionSpec as P

beta_one = 0.9
beta_two = 0.999
corr_one = 1.0 - 0.9**20
corr_two = 1.0 - 0.999**20
adam_eps = 1e-08

bf16 = jnp.bfloat16
f32 = jnp.float32
DP = ("x", "yh")
FS = ("z", "yl", "c")
ALL = DP + FS
COL = ("yh", "z", "yl")


def spread(array, axes, count):
    return lax.all_to_all(jnp.broadcast_to(array, (count,) + array.shape), axes, 0, 0)


def over_tokens(left, right):
    return lax.dot_general(left, right, (((0,), (0,)), ((), ())), preferred_element_type=f32)


def shards(inputs, grad_out, basis, moment_one, moment_two):
    basis, at_x, first = lax.optimization_barrier(
        (basis, lax.axis_index("x").astype(jnp.uint32) * 1024, lax.axis_index("c") == 0)
    )
    own_rows = spread(basis, COL, 64)
    cotangent = grad_out.T
    own_rows, cotangent = lax.optimization_barrier((own_rows, cotangent))
    slab = lax.all_gather(own_rows, "c", axis=1, tiled=True).reshape(1024, 128)
    part = lax.dynamic_slice(inputs, (jnp.uint32(0), at_x), (256, 1024))
    partial = jnp.dot(part, slab, preferred_element_type=f32).astype(bf16)
    projected = spread(partial, ("x",), 4).astype(f32).sum(0).astype(bf16)
    term = jnp.dot(cotangent, projected, preferred_element_type=f32).astype(bf16).reshape(32, 56, 128)
    even, odd = term[:, :28], term[:, 28:]
    pair = lax.all_gather(jnp.where(first, odd, even), "c", axis=0)
    term = jnp.where(first, even, odd).astype(f32) + jnp.where(first, pair[1], pair[0]).astype(f32)
    term = term.astype(bf16)
    pieces = lax.all_to_all(term, ("z", "yl"), 0, 0)
    gradient = pieces.astype(f32).sum(0)
    moment_new = beta_one * moment_one + (1.0 - beta_one) * gradient
    second_new = beta_two * moment_two + (1.0 - beta_two) * gradient * gradient
    direction = (moment_new / corr_one / (jnp.sqrt(second_new / corr_two) + adam_eps)).astype(bf16)
    near = spread(direction, ("x", "c"), 8).reshape(224, 128)
    block = lax.dot_general(
        own_rows.reshape(512, 128), near, (((1,), (1,)), ((), ())), preferred_element_type=f32
    ).astype(bf16)
    got = lax.all_to_all(block.reshape(64, 8, 224), COL, 0, 0)
    update = got.reshape(64, 8, 4, 56).transpose(1, 2, 0, 3).reshape(8, 14336)
    return (moment_new, second_new, update)


def solution(mesh):
    fine = Mesh(mesh.devices.reshape(4, 2, 8, 4, 2), ALL)
    in_specs = (P(FS, None), P(FS, DP), P(ALL, None), P(ALL, None), P(ALL, None))
    out_specs = (P(ALL, None), P(ALL, None), P(ALL, None))
    return jax.shard_map(shards, mesh=fine, in_specs=in_specs, out_specs=out_specs, check_vma=False)
```

```python
import jax
import jax.numpy as jnp
from jax import lax
from jax.sharding import Mesh, PartitionSpec as P

beta_one = 0.9
beta_two = 0.999
corr_one = 1.0 - 0.9**20
corr_two = 1.0 - 0.999**20
adam_eps = 1e-08

bf16 = jnp.bfloat16
f32 = jnp.float32
DP = ("x", "yh")
FS = ("z", "yl", "c")
ALL = DP + FS
COL = ("z", "yh", "yl")


def spread(array, axes, count):
    return lax.all_to_all(jnp.broadcast_to(array, (count,) + array.shape), axes, 0, 0)


def over_tokens(left, right):
    return lax.dot_general(left, right, (((0,), (0,)), ((), ())), preferred_element_type=f32)


def shards(inputs, grad_out, basis, moment_one, moment_two):
    basis, at_x, first = lax.optimization_barrier(
        (basis, lax.axis_index("x").astype(jnp.uint32) * 1024, lax.axis_index("c") == 0)
    )
    own_rows = spread(basis, COL, 64)
    cotangent = grad_out.T
    own_rows, cotangent = lax.optimization_barrier((own_rows, cotangent))
    slab = lax.all_gather(own_rows, "c", axis=1, tiled=True)
    slab = slab.reshape(8, 2, 64, 128).transpose(1, 0, 2, 3).reshape(1024, 128)
    part = lax.dynamic_slice(inputs, (jnp.uint32(0), at_x), (256, 1024))
    partial = jnp.dot(part, slab, preferred_element_type=f32).astype(bf16)
    projected = spread(partial, ("x",), 4).astype(f32).sum(0).astype(bf16)
    term = jnp.dot(cotangent, projected, preferred_element_type=f32).astype(bf16).reshape(32, 56, 128)
    even, odd = term[:, :28], term[:, 28:]
    pair = lax.all_gather(jnp.where(first, odd, even), "c", axis=0)
    term = jnp.where(first, even, odd).astype(f32) + jnp.where(first, pair[1], pair[0]).astype(f32)
    term = term.astype(bf16)
    pieces = lax.all_to_all(term, ("z", "yl"), 0, 0)
    gradient = pieces.astype(f32).sum(0)
    moment_new = beta_one * moment_one + (1.0 - beta_one) * gradient
    second_new = beta_two * moment_two + (1.0 - beta_two) * gradient * gradient
    direction = (moment_new / corr_one / (jnp.sqrt(second_new / corr_two) + adam_eps)).astype(bf16)
    near = spread(direction, ("x", "c"), 8).reshape(224, 128)
    block = lax.dot_general(
        own_rows.reshape(512, 128), near, (((1,), (1,)), ((), ())), preferred_element_type=f32
    ).astype(bf16)
    got = lax.all_to_all(block.reshape(64, 8, 224), ("z", "yh", "yl"), 0, 0)
    update = got.reshape(8, 2, 4, 8, 4, 56).transpose(3, 4, 1, 0, 2, 5).reshape(8, 14336)
    return (moment_new, second_new, update)


def solution(mesh):
    fine = Mesh(mesh.devices.reshape(4, 2, 8, 4, 2), ALL)
    in_specs = (P(FS, None), P(FS, DP), P(ALL, None), P(ALL, None), P(ALL, None))
    out_specs = (P(ALL, None), P(ALL, None), P(ALL, None))
    return jax.shard_map(shards, mesh=fine, in_specs=in_specs, out_specs=out_specs, check_vma=False)
```

```python
import jax
import jax.numpy as jnp
from jax import lax
from jax.experimental import pallas as pl
from jax.experimental.pallas import tpu as pltpu
from jax.sharding import Mesh, PartitionSpec as P

beta_one = 0.9
beta_two = 0.999
corr_one = 1.0 - 0.9**20
corr_two = 1.0 - 0.999**20
adam_eps = 1e-08

bf16 = jnp.bfloat16
f32 = jnp.float32
DP = ("x", "yh")
FS = ("z", "yl", "c")
ALL = DP + FS
COL = ("z", "yh", "yl")


def spread(array, axes, count):
    return lax.all_to_all(jnp.broadcast_to(array, (count,) + array.shape), axes, 0, 0)


def over_tokens(left, right):
    return lax.dot_general(left, right, (((0,), (0,)), ((), ())), preferred_element_type=f32)


def place(s):
    return s // 4 % 8 * 8 + s // 32 * 4 + s % 4


def lay_out(arrived, out_ref, got_ref, done):
    copy = pltpu.make_async_copy(arrived, got_ref, done)
    copy.start()
    copy.wait()
    lane = lax.broadcasted_iota(jnp.int32, (8, 128), 1)
    for tile in range(2):
        for group in range(4):
            parts = [got_ref[place(group * 16 + m), :, tile * 128 : tile * 128 + 128].astype(f32) for m in range(16)]
            for half in range(2):
                turned = [
                    pltpu.roll(parts[m], (m * 56 - half * 64) % 128, 1)
                    if (m * 56 - half * 64) % 128
                    else parts[m]
                    for m in range(16)
                ]
                base = (tile * 2 + half) * 3584 + group * 896
                for k in range(7):
                    low = k * 128
                    inside = [m for m in range(16) if m * 56 < low + 128 and m * 56 + 56 > low]
                    value = turned[inside[0]]
                    for m in inside[1:]:
                        value = jnp.where(lane >= m * 56 - low, turned[m], value)
                    out_ref[:, base + low : base + low + 128] = value.astype(bf16)


def shards(inputs, grad_out, basis, moment_one, moment_two):
    basis, at_x, first = lax.optimization_barrier(
        (basis, lax.axis_index("x").astype(jnp.uint32) * 1024, lax.axis_index("c") == 0)
    )
    own_rows = spread(basis, COL, 64)
    cotangent = grad_out.T
    own_rows, cotangent = lax.optimization_barrier((own_rows, cotangent))
    slab = lax.all_gather(own_rows, "c", axis=1, tiled=True)
    slab = slab.reshape(8, 2, 64, 128).transpose(1, 0, 2, 3).reshape(1024, 128)
    part = lax.dynamic_slice(inputs, (jnp.uint32(0), at_x), (256, 1024))
    partial = jnp.dot(part, slab, preferred_element_type=f32).astype(bf16)
    projected = spread(partial, ("x",), 4).astype(f32).sum(0).astype(bf16)
    term = jnp.dot(cotangent, projected, preferred_element_type=f32).astype(bf16).reshape(32, 56, 128)
    even, odd = term[:, :28], term[:, 28:]
    pair = lax.all_gather(jnp.where(first, odd, even), "c", axis=0)
    term = jnp.where(first, even, odd).astype(f32) + jnp.where(first, pair[1], pair[0]).astype(f32)
    term = term.astype(bf16)
    pieces = lax.all_to_all(term, ("z", "yl"), 0, 0)
    gradient = pieces.astype(f32).sum(0)
    moment_new = beta_one * moment_one + (1.0 - beta_one) * gradient
    second_new = beta_two * moment_two + (1.0 - beta_two) * gradient * gradient
    direction = (moment_new / corr_one / (jnp.sqrt(second_new / corr_two) + adam_eps)).astype(bf16)
    near = spread(direction, ("x", "c"), 8).reshape(4, 56, 128)
    near = jnp.pad(near, ((0, 0), (0, 8), (0, 0))).reshape(256, 128)
    block = lax.dot_general(
        own_rows.reshape(512, 128), near, (((1,), (1,)), ((), ())), preferred_element_type=f32
    ).astype(bf16)
    got = lax.all_to_all(block.reshape(64, 8, 256), COL, 0, 0)
    update = pl.pallas_call(
        lay_out,
        out_shape=jax.ShapeDtypeStruct((8, 14336), bf16),
        in_specs=[pl.BlockSpec(memory_space=pl.ANY)],
        scratch_shapes=[pltpu.VMEM((64, 8, 256), bf16), pltpu.SemaphoreType.DMA],
        compiler_params=pltpu.CompilerParams(vmem_limit_bytes=4 * 1024 * 1024),
        cost_estimate=pl.CostEstimate(flops=0, bytes_accessed=500000, transcendentals=0),
    )(got)
    return (moment_new, second_new, update)


def solution(mesh):
    fine = Mesh(mesh.devices.reshape(4, 2, 8, 4, 2), ALL)
    in_specs = (P(FS, None), P(FS, DP), P(ALL, None), P(ALL, None), P(ALL, None))
    out_specs = (P(ALL, None), P(ALL, None), P(ALL, None))
    return jax.shard_map(shards, mesh=fine, in_specs=in_specs, out_specs=out_specs, check_vma=False)
```

```python
import jax
import jax.numpy as jnp
from jax import lax
from jax.experimental import pallas as pl
from jax.experimental.pallas import tpu as pltpu
from jax.sharding import Mesh, PartitionSpec as P

beta_one = 0.9
beta_two = 0.999
corr_one = 1.0 - 0.9**20
corr_two = 1.0 - 0.999**20
adam_eps = 1e-08

bf16 = jnp.bfloat16
f32 = jnp.float32
DP = ("x", "yh")
FS = ("z", "yl", "c")
ALL = DP + FS
COL = ("z", "yh", "yl")


def spread(array, axes, count):
    return lax.all_to_all(jnp.broadcast_to(array, (count,) + array.shape), axes, 0, 0)


def over_tokens(left, right):
    return lax.dot_general(left, right, (((0,), (0,)), ((), ())), preferred_element_type=f32)


def place(s):
    return s // 4 % 8 * 8 + s // 32 * 4 + s % 4


def lay_out(arrived, out_ref, got_ref, done):
    copies = []
    for half in range(2):
        rows = pl.ds(half * 32, 32)
        copies.append(pltpu.make_async_copy(arrived.at[rows], got_ref.at[rows], done.at[half]))
        copies[half].start()
    lane = lax.broadcasted_iota(jnp.int32, (8, 128), 1)
    for group in (0, 2, 1, 3):
        if group < 2:
            copies[group].wait()
        for tile in range(2):
            parts = [got_ref[place(group * 16 + m), :, tile * 128 : tile * 128 + 128].astype(f32) for m in range(16)]
            for half in range(2):
                turned = [
                    pltpu.roll(parts[m], (m * 56 - half * 64) % 128, 1)
                    if (m * 56 - half * 64) % 128
                    else parts[m]
                    for m in range(16)
                ]
                base = (tile * 2 + half) * 3584 + group * 896
                for k in range(7):
                    low = k * 128
                    inside = [m for m in range(16) if m * 56 < low + 128 and m * 56 + 56 > low]
                    value = turned[inside[0]]
                    for m in inside[1:]:
                        value = jnp.where(lane >= m * 56 - low, turned[m], value)
                    out_ref[:, base + low : base + low + 128] = value.astype(bf16)


def shards(inputs, grad_out, basis, moment_one, moment_two):
    basis, at_x, first = lax.optimization_barrier(
        (basis, lax.axis_index("x").astype(jnp.uint32) * 1024, lax.axis_index("c") == 0)
    )
    own_rows = spread(basis, COL, 64)
    cotangent = grad_out.T
    own_rows, cotangent = lax.optimization_barrier((own_rows, cotangent))
    slab = lax.all_gather(own_rows, "c", axis=1, tiled=True)
    slab = slab.reshape(8, 2, 64, 128).transpose(1, 0, 2, 3).reshape(1024, 128)
    part = lax.dynamic_slice(inputs, (jnp.uint32(0), at_x), (256, 1024))
    partial = jnp.dot(part, slab, preferred_element_type=f32).astype(bf16)
    projected = spread(partial, ("x",), 4).astype(f32).sum(0).astype(bf16)
    term = jnp.dot(cotangent, projected, preferred_element_type=f32).astype(bf16).reshape(32, 56, 128)
    even, odd = term[:, :28], term[:, 28:]
    pair = lax.all_gather(jnp.where(first, odd, even), "c", axis=0)
    term = jnp.where(first, even, odd).astype(f32) + jnp.where(first, pair[1], pair[0]).astype(f32)
    term = term.astype(bf16)
    pieces = lax.all_to_all(term, ("z", "yl"), 0, 0)
    gradient = pieces.astype(f32).sum(0)
    moment_new = beta_one * moment_one + (1.0 - beta_one) * gradient
    second_new = beta_two * moment_two + (1.0 - beta_two) * gradient * gradient
    direction = (moment_new / corr_one / (jnp.sqrt(second_new / corr_two) + adam_eps)).astype(bf16)
    near = spread(direction, ("x", "c"), 8).reshape(4, 56, 128)
    near = jnp.pad(near, ((0, 0), (0, 8), (0, 0))).reshape(256, 128)
    block = lax.dot_general(
        own_rows.reshape(512, 128), near, (((1,), (1,)), ((), ())), preferred_element_type=f32
    ).astype(bf16)
    got = lax.all_to_all(block.reshape(64, 8, 256), COL, 0, 0)
    update = pl.pallas_call(
        lay_out,
        out_shape=jax.ShapeDtypeStruct((8, 14336), bf16),
        in_specs=[pl.BlockSpec(memory_space=pl.ANY)],
        scratch_shapes=[pltpu.VMEM((64, 8, 256), bf16), pltpu.SemaphoreType.DMA((2,))],
        compiler_params=pltpu.CompilerParams(vmem_limit_bytes=4 * 1024 * 1024),
        cost_estimate=pl.CostEstimate(flops=0, bytes_accessed=500000, transcendentals=0),
    )(got)
    return (moment_new, second_new, update)


def solution(mesh):
    fine = Mesh(mesh.devices.reshape(4, 2, 8, 4, 2), ALL)
    in_specs = (P(FS, None), P(FS, DP), P(ALL, None), P(ALL, None), P(ALL, None))
    out_specs = (P(ALL, None), P(ALL, None), P(ALL, None))
    return jax.shard_map(shards, mesh=fine, in_specs=in_specs, out_specs=out_specs, check_vma=False)
```
